256 devices in a mesh: aux: 16 (over x, y), orb: 16 (over z, core).
Axes of the slice: x: 4, y: 4, z: 8, core: 2. Of those that a mesh axis runs over, the one named last changes fastest.
Arguments:
- integrals: bfloat16 [32, 15360, 2048], P(None, 'aux', 'orb'), may hold values from -6 to 6
- coeffs: bfloat16 [2048, 2048], P('orb'), may hold values from -1 to 1
- domains: int32 [32], replicated, may hold values from 0 to 15
- eps_occ: float32 [32], replicated, may hold values from -1.5 to -0.3
- eps_vir: float32 [2048], replicated, may hold values from 0.1 to 2.5
- pair_mask: int32 [32, 32], P('aux', 'orb'), may hold values 0 or 1
Outputs:
- amplitudes: bfloat16 [32, 128, 32, 128], P('aux', None, 'orb')
- energies: float32 [32, 32], P('aux', 'orb')
The draws below stay inside these ranges and needn't reach their ends.
Inputs may be any that keep to these rules, and one draw needn't show every extreme that they name: `domains`: each entry names one of the 16 virtual blocks.
All inputs are finite; a program needn't handle non-finite values. No bound on the sum of `pair_mask` on one device may be relied on, other than what follows from the above.
Results may differ from the reference program's by a relative error of at most 0.019.
Values may be sent and summed in bfloat16 or wider, within the bound.
No kernel may reach another device: no remote copies, remote signals or barrier semaphores. Data moves between devices by JAX's collectives and lax.ppermute only.
A program may use at most 64 MiB of HBM per device.

```python
import jax
import jax.numpy as jnp
from jax import lax

NAUX = 15360
NAO = 2048
BS = 128
NVB = 16
NOCC = 32
N_ORB = 16


def draw_integrals(key, part):
    key = jax.random.fold_in(key, 11)
    shared_key, single_key = jax.random.split(key)
    shared = jnp.clip(jax.random.normal(shared_key, (NAUX, NAO), jnp.float32), -4.0, 4.0)
    single = jnp.clip(jax.random.normal(single_key, (NOCC, NAUX, NAO), jnp.float32), -4.0, 4.0)
    values = 0.7745967 * shared[None, :, :] + 0.6324555 * single
    return values.astype(jnp.bfloat16)


def draw_coeffs(key, part):
    key = jax.random.fold_in(key, 23)
    shared_key, single_key = jax.random.split(key)
    shared = jnp.clip(jax.random.normal(shared_key, (NAO, 1, BS), jnp.float32), -4.0, 4.0)
    single = jnp.clip(jax.random.normal(single_key, (NAO, NVB, BS), jnp.float32), -4.0, 4.0)
    scale = jnp.float32(NAO) ** (-0.5)
    values = (0.7416198 * shared + 0.6708204 * single) * scale
    return values.reshape(NAO, NVB * BS).astype(jnp.bfloat16)


def place_ends(values, key, low, top_value):
    longest = values.shape.index(max(values.shape))
    spots = []
    for shift in (0, 1):
        where = [jax.random.randint(jax.random.fold_in(key, axis), (), 0, length) for axis, length in enumerate(values.shape)]
        where[longest] = (where[longest] + shift) % values.shape[longest]
        spots.append(tuple(where))
    return values.at[spots[0]].set(low).at[spots[1]].set(top_value)


def setup_inputs(seed: int = 0) -> dict:
    key_list = jax.random.split(jax.random.key(seed), 7)
    return {
        "integrals": draw_integrals(jax.random.fold_in(key_list[6], 71), 0),
        "coeffs": draw_coeffs(jax.random.fold_in(key_list[6], 71), 0),
        "domains": place_ends(jax.random.randint(key_list[2], (NOCC,), 0, NVB), jax.random.fold_in(key_list[2], 1), 0, NVB - 1).astype(jnp.int32),
        "eps_occ": jnp.clip(jax.random.uniform(key_list[3], (NOCC,), jnp.float32, -1.5, -0.3), -1.5, -0.3),
        "eps_vir": jnp.clip(jax.random.uniform(key_list[4], (NVB * BS,), jnp.float32, 0.1, 2.5), 0.1, 2.5),
        "pair_mask": place_ends((jax.random.randint(key_list[5], (NOCC, NOCC), 0, 4) < 3).astype(jnp.int32), jax.random.fold_in(key_list[5], 1), 0, 1),
    }


def reference(integrals, coeffs, domains, eps_occ, eps_vir, pair_mask):
    vir_blocks = coeffs.reshape(NAO, NVB, BS)
    chosen = jnp.transpose(jnp.take(vir_blocks, domains, axis=1), (1, 0, 2))
    ao_local = NAO // N_ORB

    def add_group(orb_group, running):
        first = (orb_group * ao_local).astype(jnp.int32)
        part_ints = lax.dynamic_slice_in_dim(integrals, first, ao_local, 2).astype(jnp.float32)
        part_coef = lax.dynamic_slice_in_dim(chosen, first, ao_local, 1).astype(jnp.float32)
        partial_value = jnp.einsum('ipm,imb->ipb', part_ints, part_coef).astype(jnp.bfloat16)
        partial_value = lax.optimization_barrier(partial_value)
        return running + partial_value.astype(jnp.float32)
    running = jnp.zeros((NOCC, NAUX, BS), jnp.float32)
    running = lax.fori_loop(0, N_ORB, add_group, running)
    blocks = running.astype(jnp.bfloat16).astype(jnp.float32)
    pair_ints = jnp.einsum('jpb,ipa->jbia', blocks, blocks) * (1.0 / jnp.sqrt(jnp.float32(NAUX)))
    vir_energy = eps_vir.reshape(NVB, BS)[domains]
    denominator = vir_energy[:, :, None, None] + vir_energy[None, None, :, :] - eps_occ[:, None, None, None] - eps_occ[None, None, :, None]
    screen = pair_mask.astype(jnp.float32)
    amp = screen[:, None, :, None] * pair_ints / denominator
    energies = -lax.optimization_barrier(jnp.sum(pair_ints * amp, axis=(1, 3))) / float(BS * BS)
    return (amp.astype(jnp.bfloat16), energies)
```

```python
import jax
import jax.numpy as jnp
import numpy as np
from jax import lax
from jax.experimental import pallas as pl
from jax.experimental.pallas import tpu as pltpu
from jax.sharding import PartitionSpec as P

NAUX = 15360
BS = 128
CHIPS = 8
OWN = 4
EXTRA = 16
ROWS = 2 * BS + EXTRA
EARLY = 10
SLOTS = 16


def transform_kernel(meta, a_ref, c0, c1, c2, c3, out_ref):
    for q, c in enumerate((c0, c1, c2, c3)):
        out_ref[0, :, q * BS : (q + 1) * BS] = jnp.dot(
            a_ref[q], c[...], preferred_element_type=jnp.float32
        ).astype(jnp.bfloat16)


def combine_kernel(meta, a_ref, c0, c1, c2, c3, y_ref, out_ref):
    for q, c in enumerate((c0, c1, c2, c3)):
        lanes = slice(q * BS, (q + 1) * BS)
        total = jnp.dot(a_ref[q], c[...], preferred_element_type=jnp.float32)
        out_ref[0, :, lanes] = (total + y_ref[0, :, lanes].astype(jnp.float32)).astype(jnp.bfloat16)


def combine_split_kernel(meta, a_ref, c0, c1, c2, c3, y_ref, up_ref, down_ref):
    rows = up_ref.shape[0]
    for q, c in enumerate((c0, c1, c2, c3)):
        lanes = slice(q * BS, (q + 1) * BS)
        total = jnp.dot(a_ref[q], c[...], preferred_element_type=jnp.float32)
        total = (total + y_ref[0, :, lanes].astype(jnp.float32)).astype(jnp.bfloat16)
        up_ref[:, lanes] = total[:rows]
        down_ref[:, lanes] = total[rows:]


def chunk_call(meta, integrals, coeffs, first, count, other, received=None, split=False):
    half = integrals.shape[1] // 2
    width = OWN * BS

    def a_map(n, m):
        return (m[1 + first + n], (1 - m[0]) if other else m[0], 0)

    def c_map(q):
        return lambda n, m: (0, m[1 + CHIPS + OWN * m[1 + first + n] + q])

    in_specs = [pl.BlockSpec((OWN, half, BS), a_map)]
    in_specs += [pl.BlockSpec((BS, BS), c_map(q)) for q in range(OWN)]
    operands = [integrals] + [coeffs] * OWN
    block = pl.BlockSpec((1, half, width), lambda n, m: (n, 0, 0))
    if received is not None:
        in_specs.append(block)
        operands.append(received)
    if split:
        body = combine_split_kernel
        part = pl.BlockSpec((half // 2, width), lambda n, m: (0, 0))
        out_specs = (part, part)
        out_shape = (jax.ShapeDtypeStruct((half // 2, width), jnp.bfloat16),) * 2
    else:
        body = transform_kernel if received is None else combine_kernel
        out_specs = block
        out_shape = jax.ShapeDtypeStruct((count, half, width), jnp.bfloat16)
    return pl.pallas_call(
        body,
        grid_spec=pltpu.PrefetchScalarGridSpec(
            num_scalar_prefetch=1, grid=(count,), in_specs=in_specs, out_specs=out_specs
        ),
        out_shape=out_shape,
        compiler_params=pltpu.CompilerParams(vmem_limit_bytes=32 * 2**20),
    )(meta, *operands)


def gram(left, right):
    return lax.dot_general(
        left, right, (((0,), (0,)), ((), ())), preferred_element_type=jnp.float32
    )


def orbital(ref, index):
    return ref[:, pl.ds(pl.multiple_of(index * BS, BS), BS)]


def put(out_ref, slot, product, received):
    for m in range(2):
        value = product[:, m * BS : (m + 1) * BS]
        if received is not None:
            value = value + received[slot, m * BS : (m + 1) * BS].astype(jnp.float32)
        out_ref[slot, m * BS : (m + 1) * BS] = value.astype(jnp.bfloat16)
    out_ref[slot, 2 * BS :] = jnp.zeros((EXTRA, BS), jnp.bfloat16)


def block_products(h, left_ref, right_ref, slot, out_ref, received):
    left = jnp.concatenate([orbital(left_ref, h), orbital(left_ref, 2 + h)], axis=1)
    product = gram(left, right_ref[...])
    for l in range(2):
        for m in range(2):
            piece = product[l * BS : (l + 1) * BS, 2 * m * BS : 2 * (m + 1) * BS]
            put(out_ref, slot + 2 * l + m, piece, received)


def early_kernel(other, meta, own_ref, prev_ref, next_ref, *refs):
    received, out_ref = refs if len(refs) == 2 else (None, refs[0])
    h = (1 - meta[0]) if other else meta[0]
    block_products(h, own_ref, next_ref, 0, out_ref, received)
    block_products(h, prev_ref, next_ref, 4, out_ref, received)
    put(out_ref, 8, gram(orbital(own_ref, h), own_ref[:, 2 * BS :]), received)
    pair = jnp.concatenate([orbital(own_ref, 2 * h), orbital(own_ref, 2 * h + 1)], axis=1)
    diag = gram(pair, pair)
    row = lax.broadcasted_iota(jnp.int32, (BS, BS), 0)
    col = lax.broadcasted_iota(jnp.int32, (BS, BS), 1)
    second = diag[BS:, BS:]
    packed = jnp.where(row >= col, diag[:BS, :BS], second)
    line = jnp.sum(jnp.where(row == col, second, 0.0), axis=0, keepdims=True)
    line = jnp.broadcast_to(line, (EXTRA, BS))
    cross = diag[:BS, BS:]
    if received is not None:
        packed = packed + received[9, :BS].astype(jnp.float32)
        cross = cross + received[9, BS : 2 * BS].astype(jnp.float32)
        line = line + received[9, 2 * BS :].astype(jnp.float32)
    out_ref[9, :BS] = packed.astype(jnp.bfloat16)
    out_ref[9, BS : 2 * BS] = cross.astype(jnp.bfloat16)
    out_ref[9, 2 * BS :] = line.astype(jnp.bfloat16)


def late_products(h, chip, prev_ref, next2_ref, prev2_ref, slot, out_ref, received):
    block_products(h, prev_ref, next2_ref, slot, out_ref, received)

    def opposite(left, right):
        product = gram(left, right[...])
        for m in range(2):
            put(out_ref, slot + 4 + m, product[:, 2 * m * BS : 2 * (m + 1) * BS], received)

    @pl.when(chip < CHIPS // 2)
    def _():
        opposite(orbital(prev2_ref, h), next2_ref)

    @pl.when(chip >= CHIPS // 2)
    def _():
        opposite(orbital(next2_ref, 2 + h), prev2_ref)


def late_send_kernel(meta, prev_ref, next2_ref, prev2_ref, out_ref):
    late_products(1 - meta[0], meta[1], prev_ref, next2_ref, prev2_ref, 0, out_ref, None)


class Shifted:
    def __init__(self, ref, by):
        self.ref, self.by = ref, by

    def __getitem__(self, key):
        return self.ref[(key[0] - self.by,) + key[1:]]


def late_own_kernel(meta, prev_ref, next2_ref, prev2_ref, early_ref, received, out_ref):
    out_ref[:EARLY] = early_ref[...]
    late_products(
        meta[0], meta[1], prev_ref, next2_ref, prev2_ref, EARLY, out_ref, Shifted(received, EARLY)
    )


def pair_call(body, meta, operands, slots):
    return pl.pallas_call(
        body,
        grid_spec=pltpu.PrefetchScalarGridSpec(
            num_scalar_prefetch=1,
            grid=(1,),
            in_specs=[
                pl.BlockSpec(x.shape, lambda n, m, nd=x.ndim: (0,) * nd) for x in operands
            ],
            out_specs=pl.BlockSpec((slots, ROWS, BS), lambda n, m: (0, 0, 0)),
        ),
        out_shape=jax.ShapeDtypeStruct((slots, ROWS, BS), jnp.bfloat16),
        compiler_params=pltpu.CompilerParams(vmem_limit_bytes=32 * 2**20),
    )(meta, *operands)


def final_kernel(meta, eps_occ, mask, first_ref, second_ref, vir_ref, amp_ref, energy_ref, t_ref):
    kind = meta[0]
    units = [slice(0, BS), slice(BS, 2 * BS)]

    @pl.when(kind == 0)
    def _():
        for j, ref in enumerate((first_ref, second_ref)):
            for i in range(2):
                t_ref[j, i] = ref[units[i]].astype(jnp.float32)

    @pl.when(kind == 1)
    def _():
        for i, ref in enumerate((second_ref, first_ref)):
            for j in range(2):
                t_ref[j, i] = ref[units[j]].astype(jnp.float32).T

    @pl.when(kind == 2)
    def _():
        row = lax.broadcasted_iota(jnp.int32, (BS, BS), 0)
        col = lax.broadcasted_iota(jnp.int32, (BS, BS), 1)
        packed = first_ref[units[0]].astype(jnp.float32)
        flipped = packed.T
        line = first_ref[2 * BS : 2 * BS + EXTRA].astype(jnp.float32)[:1]
        t_ref[0, 0] = jnp.where(row >= col, packed, flipped)
        t_ref[1, 1] = jnp.where(row < col, packed, jnp.where(row > col, flipped, line))
        cross = first_ref[units[1]].astype(jnp.float32)
        t_ref[0, 1] = cross
        t_ref[1, 0] = cross.T

    scale = 1.0 / np.sqrt(np.float32(NAUX))
    for j in range(2):
        jj = 2 * meta[1] + j
        vir_j = vir_ref[pl.ds(meta[3 + jj], 1), :]
        rows = jnp.broadcast_to(vir_j, (BS, BS)).T
        for i in range(2):
            ii = 2 * meta[2] + i
            vir_i = vir_ref[pl.ds(meta[3 + ii], 1), :]
            denominator = rows + vir_i - eps_occ[jj] - eps_occ[ii]
            pair = t_ref[j, i] * scale
            keep = mask[j, i].astype(jnp.float32)
            amp = keep * pair / denominator
            amp_ref[j, :, i * BS : (i + 1) * BS] = amp.astype(jnp.bfloat16)
            energy = jnp.sum(jnp.sum(pair * amp, axis=1, keepdims=True), axis=0, keepdims=True)
            energy_ref[2 * j + i : 2 * j + i + 1] = jnp.broadcast_to(
                energy * (-1.0 / (BS * BS)), (1, BS)
            )


def final_call(meta, eps_occ, mask, first, second, vir):
    return pl.pallas_call(
        final_kernel,
        grid_spec=pltpu.PrefetchScalarGridSpec(
            num_scalar_prefetch=3,
            grid=(1,),
            in_specs=[
                pl.BlockSpec(first.shape, lambda n, *m: (0, 0)),
                pl.BlockSpec(second.shape, lambda n, *m: (0, 0)),
                pl.BlockSpec(vir.shape, lambda n, *m: (0, 0)),
            ],
            out_specs=(
                pl.BlockSpec((2, BS, 2 * BS), lambda n, *m: (0, 0, 0)),
                pl.BlockSpec((8, BS), lambda n, *m: (0, 0)),
            ),
            scratch_shapes=[pltpu.VMEM((2, 2, BS, BS), jnp.float32)],
        ),
        out_shape=(
            jax.ShapeDtypeStruct((2, BS, 2 * BS), jnp.bfloat16),
            jax.ShapeDtypeStruct((8, BS), jnp.float32),
        ),
    )(meta, eps_occ, mask, first, second, vir)


def slot_pairs(chip):
    sup = lambda off, l: 2 * ((chip + off) % CHIPS) + l
    pairs = [(sup(0, l), sup(1, m)) for l in range(2) for m in range(2)]
    pairs += [(sup(-1, l), sup(1, m)) for l in range(2) for m in range(2)]
    pairs += [(sup(0, 0), sup(0, 1)), None]
    pairs += [(sup(-1, l), sup(2, m)) for l in range(2) for m in range(2)]
    if chip < CHIPS // 2:
        pairs += [(sup(-2, 0), sup(2, m)) for m in range(2)]
    else:
        pairs += [(sup(2, 1), sup(-2, m)) for m in range(2)]
    return pairs


def delivery():
    rounds = ([], [])
    kind = np.full((SLOTS, SLOTS), -1, np.int32)
    for chip in range(CHIPS):
        for slot, pair in enumerate(slot_pairs(chip)):
            source = [slot * SLOTS + 2 * chip + core for core in range(2)]
            if pair is None:
                for core in range(2):
                    o = 2 * chip + core
                    rounds[0].append((source[core], o * SLOTS + o))
                    kind[o, o] = 2
                continue
            u, v = pair
            owners = [u * SLOTS + v, v * SLOTS + u]
            kind[u, v], kind[v, u] = 0, 1
            rounds[0].extend([(source[0], owners[0]), (source[1], owners[1])])
            rounds[1].extend([(source[0], owners[1]), (source[1], owners[0])])
    assert (kind >= 0).all()
    return rounds, kind


def shards(integrals, coeffs, domains, eps_occ, eps_vir, pair_mask):
    aux = lax.axis_index("aux")
    orb = lax.axis_index("orb")
    chip = orb // 2
    core = orb % 2
    half = integrals.shape[1] // 2
    quarter = half // 2

    n_orb = 2 * CHIPS
    swap = lambda x: lax.ppermute(x, "orb", [(o, o ^ 1) for o in range(n_orb)])
    up = lambda x: lax.ppermute(x, "orb", [(o, (o + 2) % n_orb) for o in range(n_orb)])
    down = lambda x: lax.ppermute(x, "orb", [(o, (o - 2) % n_orb) for o in range(n_orb)])

    order = jnp.array([4, 3, 5, 2, 6, 1, 7, 0], jnp.int32)
    meta = jnp.concatenate([core[None], (order + chip) % CHIPS, domains]).astype(jnp.int32)

    def combined(first, count, split=False):
        send = chunk_call(meta, integrals, coeffs, first, count, True)
        return chunk_call(meta, integrals, coeffs, first, count, False, swap(send), split)

    start_up, start_down = combined(0, 1, True)
    x1 = combined(1, 2)
    x2 = combined(3, 5)
    up_sum, down_sum = up(start_up), down(start_down)
    up_sum = jnp.concatenate([x1[0, :quarter] + up_sum, x1[0, quarter:]], axis=0)
    down_sum = jnp.concatenate([x1[1, :quarter], x1[1, quarter:] + down_sum], axis=0)
    for step in range(2):
        up_sum, down_sum = up(up_sum), down(down_sum)
        up_sum = x2[2 * step] + up_sum
        down_sum = x2[2 * step + 1] + down_sum
    up_sum, down_sum = up(up_sum), down(down_sum)
    f32 = jnp.float32
    own = (x2[4].astype(f32) + up_sum.astype(f32) + down_sum.astype(f32)).astype(jnp.bfloat16)

    prev, next_ = up(own), down(own)
    prev2, next2 = up(prev), down(next_)

    where = jnp.stack([core, chip]).astype(jnp.int32)
    send = pair_call(lambda *r: early_kernel(True, *r), where, (own, prev, next_), EARLY)
    early = pair_call(
        lambda *r: early_kernel(False, *r), where, (own, prev, next_, swap(send)), EARLY
    )
    send = pair_call(late_send_kernel, where, (prev, next2, prev2), SLOTS - EARLY)
    sums = pair_call(
        late_own_kernel, where, (prev, next2, prev2, early, swap(send)), SLOTS
    )
    parts = lax.all_to_all(sums, "aux", 0, 0, tiled=True)
    held = jnp.sum(parts.astype(f32), axis=0).astype(jnp.bfloat16)

    rounds, kind = delivery()
    first = lax.ppermute(held, ("aux", "orb"), rounds[0])
    second = lax.ppermute(held, ("aux", "orb"), rounds[1])
    info = jnp.stack([jnp.asarray(kind)[aux, orb], aux, orb]).astype(jnp.int32)
    amplitudes, energies = final_call(
        jnp.concatenate([info, domains]),
        eps_occ,
        pair_mask,
        first,
        second,
        eps_vir.reshape(-1, BS),
    )
    return amplitudes.reshape(2, BS, 2, BS), energies[:4, 0].reshape(2, 2)


def solution(mesh):
    return jax.shard_map(
        shards,
        mesh=mesh,
        in_specs=(P(None, "aux", "orb"), P("orb", None), P(), P(), P(), P("aux", "orb")),
        out_specs=(P("aux", None, "orb", None), P("aux", "orb")),
        check_vma=False,
    )
```

```python
import functools

import jax
import jax.numpy as jnp
import numpy as np
from jax import lax
from jax.experimental import pallas as pl
from jax.experimental.pallas import tpu as pltpu
from jax.sharding import PartitionSpec as P

NAUX = 15360
BS = 128
CHIPS = 8
OWN = 4
EXTRA = 16
ROWS = 2 * BS + EXTRA
EARLY = 10
SLOTS = 16
RINGS = 2
TRANSFORM_VMEM = 24 * 2**20
PAIR_VMEM = 32 * 2**20


def transform_rows(out_ref, rows, a_at, coeff_at):
    for q in range(OWN):
        out_ref[:, q * BS : (q + 1) * BS] = jnp.dot(
            a_at(q, rows), coeff_at(q), preferred_element_type=jnp.float32
        ).astype(out_ref.dtype)


def core_halves():
    core = lax.axis_index("orb") % 2
    return 1 - core, core


def transform_kernel(firsts, domains, a_hbm, c_hbm, send_ref, own_ref, a_ref, c_ref, sems):
    copies = []
    for n, first in enumerate(firsts):
        chunk = (lax.axis_index("orb") // 2 + first) % CHIPS
        here = []
        for q in range(OWN):
            lanes = pl.ds(pl.multiple_of(domains[OWN * chunk + q] * BS, BS), BS)
            here.append((c_hbm.at[:, lanes], c_ref.at[n, q]))
        for side, half in enumerate(core_halves()):
            here.append((a_hbm.at[pl.ds(OWN * chunk, OWN), half], a_ref.at[n, side]))
        copies.append(
            [pltpu.make_async_copy(x, y, sems.at[n, k]) for k, (x, y) in enumerate(here)]
        )
        for copy in copies[-1]:
            copy.start()
    for n in range(len(firsts)):
        for copy in copies[n][:-1]:
            copy.wait()
        transform_rows(send_ref.at[n], 0, lambda q, side: a_ref[n, side, q], lambda q: c_ref[n, q])
        copies[n][-1].wait()
        transform_rows(own_ref.at[n], 1, lambda q, side: a_ref[n, side, q], lambda q: c_ref[n, q])


def transform_call(domains, integrals, coeffs, firsts):
    half, width, count = integrals.shape[2], OWN * BS, len(firsts)
    hbm = pl.BlockSpec(memory_space=pltpu.HBM)
    vmem = pl.BlockSpec(memory_space=pltpu.VMEM)
    return pl.pallas_call(
        functools.partial(transform_kernel, firsts),
        in_specs=[pl.BlockSpec(memory_space=pltpu.SMEM), hbm, hbm],
        out_specs=(vmem, vmem),
        scratch_shapes=[
            pltpu.VMEM((count, 2, OWN, half, BS), jnp.bfloat16),
            pltpu.VMEM((count, OWN, BS, BS), jnp.bfloat16),
            pltpu.SemaphoreType.DMA((count, OWN + 2)),
        ],
        out_shape=(
            jax.ShapeDtypeStruct((count, half, width), jnp.bfloat16),
            jax.ShapeDtypeStruct((count, half, width), jnp.float32),
        ),
        cost_estimate=pl.CostEstimate(
            flops=4 * count * half * width * BS,
            bytes_accessed=count * half * (4 * width + 6 * width),
            transcendentals=0,
        ),
        compiler_params=pltpu.CompilerParams(vmem_limit_bytes=TRANSFORM_VMEM),
    )(domains, integrals, coeffs)


def gram(left, right):
    return lax.dot_general(
        left, right, (((0,), (0,)), ((), ())), preferred_element_type=jnp.float32
    )


def orbital(ref, index):
    return ref[:, pl.ds(pl.multiple_of(index * BS, BS), BS)]


def put(out_ref, slot, product, received):
    for m in range(2):
        value = product[:, m * BS : (m + 1) * BS]
        if received is not None:
            value = value + received[slot, m * BS : (m + 1) * BS].astype(jnp.float32)
        out_ref[slot, m * BS : (m + 1) * BS] = value.astype(jnp.bfloat16)
    out_ref[slot, 2 * BS :] = jnp.zeros((EXTRA, BS), jnp.bfloat16)


def block_products(h, left_ref, right_ref, slot, out_ref, received):
    left = jnp.concatenate([orbital(left_ref, h), orbital(left_ref, 2 + h)], axis=1)
    product = gram(left, right_ref[...])
    for l in range(2):
        for m in range(2):
            piece = product[l * BS : (l + 1) * BS, 2 * m * BS : 2 * (m + 1) * BS]
            put(out_ref, slot + 2 * l + m, piece, received)


def early_kernel(other, own_ref, prev_ref, next_ref, *refs):
    received, out_ref = refs if len(refs) == 2 else (None, refs[0])
    core = lax.axis_index("orb") % 2
    h = 1 - core if other else core
    block_products(h, own_ref, next_ref, 0, out_ref, received)
    block_products(h, prev_ref, next_ref, 4, out_ref, received)
    put(out_ref, 8, gram(orbital(own_ref, h), own_ref[:, 2 * BS :]), received)
    pair = jnp.concatenate([orbital(own_ref, 2 * h), orbital(own_ref, 2 * h + 1)], axis=1)
    diag = gram(pair, pair)
    row = lax.broadcasted_iota(jnp.int32, (BS, BS), 0)
    col = lax.broadcasted_iota(jnp.int32, (BS, BS), 1)
    second = diag[BS:, BS:]
    packed = jnp.where(row >= col, diag[:BS, :BS], second)
    line = jnp.sum(jnp.where(row == col, second, 0.0), axis=0, keepdims=True)
    line = jnp.broadcast_to(line, (EXTRA, BS))
    cross = diag[:BS, BS:]
    if received is not None:
        packed = packed + received[9, :BS].astype(jnp.float32)
        cross = cross + received[9, BS : 2 * BS].astype(jnp.float32)
        line = line + received[9, 2 * BS :].astype(jnp.float32)
    out_ref[9, :BS] = packed.astype(jnp.bfloat16)
    out_ref[9, BS : 2 * BS] = cross.astype(jnp.bfloat16)
    out_ref[9, 2 * BS :] = line.astype(jnp.bfloat16)


def late_products(other, prev_ref, next2_ref, prev2_ref, slot, out_ref, received):
    core = lax.axis_index("orb") % 2
    chip = lax.axis_index("orb") // 2
    h = 1 - core if other else core
    block_products(h, prev_ref, next2_ref, slot, out_ref, received)

    def opposite(left, right):
        product = gram(left, right[...])
        for m in range(2):
            put(out_ref, slot + 4 + m, product[:, 2 * m * BS : 2 * (m + 1) * BS], received)

    @pl.when(chip < CHIPS // 2)
    def _():
        opposite(orbital(prev2_ref, h), next2_ref)

    @pl.when(chip >= CHIPS // 2)
    def _():
        opposite(orbital(next2_ref, 2 + h), prev2_ref)


def late_send_kernel(prev_ref, next2_ref, prev2_ref, out_ref):
    late_products(True, prev_ref, next2_ref, prev2_ref, 0, out_ref, None)


class Shifted:
    def __init__(self, ref, by):
        self.ref, self.by = ref, by

    def __getitem__(self, key):
        return self.ref[(key[0] - self.by,) + key[1:]]


def late_own_kernel(prev_ref, next2_ref, prev2_ref, early_ref, received, out_ref):
    out_ref[:EARLY] = early_ref[...]
    late_products(
        False, prev_ref, next2_ref, prev2_ref, EARLY, out_ref, Shifted(received, EARLY)
    )


def pair_call(body, operands, slots):
    return pl.pallas_call(
        body,
        out_shape=jax.ShapeDtypeStruct((slots, ROWS, BS), jnp.bfloat16),
        compiler_params=pltpu.CompilerParams(vmem_limit_bytes=PAIR_VMEM),
    )(*operands)


def final_kernel(kinds, domains, eps_occ, mask, both_ref, vir_ref, amp_ref, energy_ref, t_ref):
    first_ref, second_ref = both_ref.at[:ROWS], both_ref.at[ROWS:]
    aux = lax.axis_index("aux")
    orb = lax.axis_index("orb")
    kind = kinds[aux, orb]
    units = [slice(0, BS), slice(BS, 2 * BS)]

    @pl.when(kind == 0)
    def _():
        for j, ref in enumerate((first_ref, second_ref)):
            for i in range(2):
                t_ref[j, i] = ref[units[i]].astype(jnp.float32)

    @pl.when(kind == 1)
    def _():
        for i, ref in enumerate((second_ref, first_ref)):
            for j in range(2):
                t_ref[j, i] = ref[units[j]].astype(jnp.float32).T

    @pl.when(kind == 2)
    def _():
        row = lax.broadcasted_iota(jnp.int32, (BS, BS), 0)
        col = lax.broadcasted_iota(jnp.int32, (BS, BS), 1)
        packed = first_ref[units[0]].astype(jnp.float32)
        flipped = packed.T
        line = first_ref[2 * BS : 2 * BS + EXTRA].astype(jnp.float32)[:1]
        t_ref[0, 0] = jnp.where(row >= col, packed, flipped)
        t_ref[1, 1] = jnp.where(row < col, packed, jnp.where(row > col, flipped, line))
        cross = first_ref[units[1]].astype(jnp.float32)
        t_ref[0, 1] = cross
        t_ref[1, 0] = cross.T

    scale = 1.0 / np.sqrt(np.float32(NAUX))
    for j in range(2):
        jj = 2 * aux + j
        vir_j = vir_ref[pl.ds(domains[jj], 1), :]
        rows = jnp.broadcast_to(vir_j, (BS, BS)).T
        amps = []
        for i in range(2):
            ii = 2 * orb + i
            vir_i = vir_ref[pl.ds(domains[ii], 1), :]
            denominator = rows + vir_i - eps_occ[jj] - eps_occ[ii]
            pair = t_ref[j, i] * scale
            keep = mask[j, i].astype(jnp.float32)
            amp = keep * pair / denominator
            amps.append(amp)
            energy_ref[j, i] = jnp.sum(pair * amp) * (-1.0 / (BS * BS))
        amp_ref[j] = jnp.stack(amps, axis=1).astype(jnp.bfloat16)


def final_call(kinds, domains, eps_occ, mask, both, vir):
    return pl.pallas_call(
        final_kernel,
        grid_spec=pltpu.PrefetchScalarGridSpec(
            num_scalar_prefetch=4,
            grid=(1,),
            in_specs=[
                pl.BlockSpec(both.shape, lambda n, *m: (0, 0)),
                pl.BlockSpec(vir.shape, lambda n, *m: (0, 0)),
            ],
            out_specs=(
                pl.BlockSpec((2, BS, 2, BS), lambda n, *m: (0, 0, 0, 0)),
                pl.BlockSpec(memory_space=pltpu.SMEM),
            ),
            scratch_shapes=[pltpu.VMEM((2, 2, BS, BS), jnp.float32)],
        ),
        out_shape=(
            jax.ShapeDtypeStruct((2, BS, 2, BS), jnp.bfloat16),
            jax.ShapeDtypeStruct((2, 2), jnp.float32),
        ),
        compiler_params=pltpu.CompilerParams(vmem_limit_bytes=PAIR_VMEM),
    )(kinds, domains, eps_occ, mask, both, vir)


def slot_pairs(chip):
    sup = lambda off, l: 2 * ((chip + off) % CHIPS) + l
    pairs = [(sup(0, l), sup(1, m)) for l in range(2) for m in range(2)]
    pairs += [(sup(-1, l), sup(1, m)) for l in range(2) for m in range(2)]
    pairs += [(sup(0, 0), sup(0, 1)), None]
    pairs += [(sup(-1, l), sup(2, m)) for l in range(2) for m in range(2)]
    if chip < CHIPS // 2:
        pairs += [(sup(-2, 0), sup(2, m)) for m in range(2)]
    else:
        pairs += [(sup(2, 1), sup(-2, m)) for m in range(2)]
    return pairs


def delivery():
    pairs = []
    kind = np.full((SLOTS, SLOTS), -1, np.int32)
    for chip in range(CHIPS):
        for slot, pair in enumerate(slot_pairs(chip)):
            for core in range(2):
                u, v = pair or (2 * chip + core,) * 2
                owner = (v, u) if core else (u, v)
                pairs.append((slot * SLOTS + 2 * chip + core, owner[0] * SLOTS + owner[1]))
                kind[owner] = core if pair else 2
    assert (kind >= 0).all()
    return pairs, kind


def shards(integrals, coeffs, domains, eps_occ, eps_vir, pair_mask):
    f32 = jnp.float32
    half = integrals.shape[1] // 2
    integrals = integrals.reshape(-1, 2, half, BS)
    n_orb = 2 * CHIPS
    tie = lax.optimization_barrier
    swap = lambda x: lax.ppermute(x, "orb", [(o, o ^ 1) for o in range(n_orb)])
    up = lambda x: lax.ppermute(x, "orb", [(o, (o + 2) % n_orb) for o in range(n_orb)])
    down = lambda x: lax.ppermute(x, "orb", [(o, (o - 2) % n_orb) for o in range(n_orb)])

    part = half // RINGS
    terms = {}

    def after(x, *others):
        return tie((x, *others))[0]

    def transform(firsts, *others):
        send, mine = transform_call(domains, after(integrals, *others), coeffs, firsts)
        theirs = swap(send)
        values = [
            mine[n, first : first + part] + theirs[n, first : first + part].astype(f32)
            for n in range(len(firsts))
            for first in range(0, half, part)
        ]
        if len(firsts) > 1:
            values = tie(values)
        terms.update({k: values[RINGS * n : RINGS * (n + 1)] for n, k in enumerate(firsts)})
        return send

    def add(x, *received):
        return sum((r.astype(f32) for r in received), x).astype(jnp.bfloat16)

    send = transform((4,))
    send = transform((3, 5), send)
    transform((2, 6, 1, 7, 0), send)
    h = part // 2
    starts = [tie((add(x[:h]), add(x[h:]))) for x in terms[4]]
    sums = [(up(u), down(d)) for u, d in starts]
    for step in (3, 2, 1):
        later = []
        for n, (u, d) in enumerate(sums):
            x, y = terms[step][n], terms[CHIPS - step][n]
            if step == 3:
                u = jnp.concatenate([add(x[:h], u), add(x[h:])], axis=0)
                d = jnp.concatenate([add(y[:h]), add(y[h:], d)], axis=0)
            else:
                u, d = add(x, u), add(y, d)
            u, d = tie((u, d))
            later.append((up(u), down(d)))
        sums = later
    own, prev, next_, prev2, next2 = [], [], [], [], []
    for n, (u, d) in enumerate(sums):
        own.append(tie(add(terms[0][n], u, d)))
        prev.append(up(own[-1]))
        next_.append(down(own[-1]))
    for n in range(RINGS):
        u, d = tie((prev[n], next_[n]))
        prev2.append(up(u))
        next2.append(down(d))
    own, prev, next_, prev2, next2 = (
        jnp.concatenate(x, axis=0) for x in (own, prev, next_, prev2, next2)
    )

    send = pair_call(functools.partial(early_kernel, True), (own, prev, next_), EARLY)
    early = pair_call(
        functools.partial(early_kernel, False), (own, prev, next_, swap(send)), EARLY
    )
    send = pair_call(late_send_kernel, (prev, next2, prev2), SLOTS - EARLY)
    sums = pair_call(late_own_kernel, (prev, next2, prev2, early, swap(send)), SLOTS)
    parts = lax.all_to_all(sums.reshape(SLOTS * ROWS, BS), "aux", 0, 0, tiled=True)
    held = jnp.sum(parts.reshape(SLOTS, ROWS, BS).astype(f32), axis=0).astype(jnp.bfloat16)
    both = jnp.concatenate([held, swap(held)], axis=0)
    pairs, kind = delivery()
    both = lax.ppermute(both, ("aux", "orb"), pairs)
    return final_call(
        jnp.asarray(kind), domains, eps_occ, pair_mask, both, eps_vir.reshape(-1, BS)
    )


def solution(mesh):
    return jax.shard_map(
        shards,
        mesh=mesh,
        in_specs=(P(None, "aux", "orb"), P("orb", None), P(), P(), P(), P("aux", "orb")),
        out_specs=(P("aux", None, "orb", None), P("aux", "orb")),
        check_vma=False,
    )
```

```python
import functools

import jax
import jax.numpy as jnp
import numpy as np
from jax import lax
from jax.experimental import pallas as pl
from jax.experimental.pallas import tpu as pltpu
from jax.sharding import PartitionSpec as P

NAUX = 15360
BS = 128
CHIPS = 8
OWN = 4
EXTRA = 16
ROWS = 2 * BS + EXTRA
EARLY = 10
SLOTS = 16
RINGS = 2
TRANSFORM_VMEM = 57 * 2**20
GROUPS = (1, 2, 5)
PAIR_VMEM = 32 * 2**20


def transform_kernel(order, domains, a_hbm, c_hbm, *refs):
    outs, (a_ref, c_ref, out_ref, sems, out_sems) = refs[:-5], refs[-5:]
    chip, core = lax.axis_index("orb") // 2, lax.axis_index("orb") % 2
    chunks = [(chip + distance) % CHIPS for distance in order]
    places = [(g, n) for g, count in enumerate(GROUPS) for n in range(count)]
    copies = [pltpu.make_async_copy(c_hbm, c_ref, sems.at[len(order)])]
    copies += [
        pltpu.make_async_copy(a_hbm.at[pl.ds(OWN * chunk, OWN)], a_ref.at[n], sems.at[n])
        for n, chunk in enumerate(chunks)
    ]
    for copy in copies:
        copy.start()
    copies[0].wait()
    zeros = jnp.zeros((BS, BS), jnp.bfloat16)
    results = []
    for n, chunk in enumerate(chunks):
        copies[1 + n].wait()
        group, index = places[n]
        for q in range(0, OWN, 2):
            c0, c1 = (
                c_ref[:, pl.ds(pl.multiple_of(domains[OWN * chunk + q + k] * BS, BS), BS)]
                for k in range(2)
            )
            chosen = jnp.concatenate(
                [jnp.concatenate([c0, zeros], 1), jnp.concatenate([zeros, c1], 1)], 0
            )
            for side, half in enumerate((1 - core, core)):
                left = jnp.concatenate([a_ref[n, q, half], a_ref[n, q + 1, half]], 1)
                out_ref[n, side, :, q * BS : (q + 2) * BS] = jnp.dot(
                    left, chosen, preferred_element_type=jnp.float32
                ).astype(jnp.bfloat16)
        for side in range(2):
            results.append(
                pltpu.make_async_copy(
                    out_ref.at[n, side], outs[2 * group + side].at[index], out_sems.at[n, side]
                )
            )
            results[-1].start()
    for result in results:
        result.wait()


def transform_call(domains, integrals, coeffs, order):
    half, width, count = integrals.shape[2], OWN * BS, len(order)
    hbm = pl.BlockSpec(memory_space=pltpu.HBM)
    outs = [jax.ShapeDtypeStruct((n, half, width), jnp.bfloat16) for n in GROUPS for _ in range(2)]
    return pl.pallas_call(
        functools.partial(transform_kernel, order),
        in_specs=[pl.BlockSpec(memory_space=pltpu.SMEM), hbm, hbm],
        out_specs=(hbm,) * len(outs),
        scratch_shapes=[
            pltpu.VMEM((count, OWN, 2, half, BS), jnp.bfloat16),
            pltpu.VMEM(coeffs.shape, jnp.bfloat16),
            pltpu.VMEM((count, 2, half, width), jnp.bfloat16),
            pltpu.SemaphoreType.DMA((count + 1,)),
            pltpu.SemaphoreType.DMA((count, 2)),
        ],
        out_shape=tuple(outs),
        compiler_params=pltpu.CompilerParams(vmem_limit_bytes=TRANSFORM_VMEM),
    )(domains, integrals, coeffs)


def gram(left, right):
    return lax.dot_general(
        left, right, (((0,), (0,)), ((), ())), preferred_element_type=jnp.float32
    )


def orbital(ref, index):
    return ref[:, pl.ds(pl.multiple_of(index * BS, BS), BS)]


def put(out_ref, slot, product, received):
    for m in range(2):
        value = product[:, m * BS : (m + 1) * BS]
        if received is not None:
            value = value + received[slot, m * BS : (m + 1) * BS].astype(jnp.float32)
        out_ref[slot, m * BS : (m + 1) * BS] = value.astype(jnp.bfloat16)
    out_ref[slot, 2 * BS :] = jnp.zeros((EXTRA, BS), jnp.bfloat16)


def block_products(h, left_ref, right_ref, slot, out_ref, received):
    left = jnp.concatenate([orbital(left_ref, h), orbital(left_ref, 2 + h)], axis=1)
    product = gram(left, right_ref[...])
    for l in range(2):
        for m in range(2):
            piece = product[l * BS : (l + 1) * BS, 2 * m * BS : 2 * (m + 1) * BS]
            put(out_ref, slot + 2 * l + m, piece, received)


def early_kernel(other, own_ref, prev_ref, next_ref, *refs):
    received, out_ref = refs if len(refs) == 2 else (None, refs[0])
    core = lax.axis_index("orb") % 2
    h = 1 - core if other else core
    block_products(h, own_ref, next_ref, 0, out_ref, received)
    block_products(h, prev_ref, next_ref, 4, out_ref, received)
    put(out_ref, 8, gram(orbital(own_ref, h), own_ref[:, 2 * BS :]), received)
    pair = jnp.concatenate([orbital(own_ref, 2 * h), orbital(own_ref, 2 * h + 1)], axis=1)
    diag = gram(pair, pair)
    row = lax.broadcasted_iota(jnp.int32, (BS, BS), 0)
    col = lax.broadcasted_iota(jnp.int32, (BS, BS), 1)
    second = diag[BS:, BS:]
    packed = jnp.where(row >= col, diag[:BS, :BS], second)
    line = jnp.sum(jnp.where(row == col, second, 0.0), axis=0, keepdims=True)
    line = jnp.broadcast_to(line, (EXTRA, BS))
    cross = diag[:BS, BS:]
    if received is not None:
        packed = packed + received[9, :BS].astype(jnp.float32)
        cross = cross + received[9, BS : 2 * BS].astype(jnp.float32)
        line = line + received[9, 2 * BS :].astype(jnp.float32)
    out_ref[9, :BS] = packed.astype(jnp.bfloat16)
    out_ref[9, BS : 2 * BS] = cross.astype(jnp.bfloat16)
    out_ref[9, 2 * BS :] = line.astype(jnp.bfloat16)


def late_products(other, prev_ref, next2_ref, prev2_ref, slot, out_ref, received):
    core = lax.axis_index("orb") % 2
    chip = lax.axis_index("orb") // 2
    h = 1 - core if other else core
    block_products(h, prev_ref, next2_ref, slot, out_ref, received)

    def opposite(left, right):
        product = gram(left, right[...])
        for m in range(2):
            put(out_ref, slot + 4 + m, product[:, 2 * m * BS : 2 * (m + 1) * BS], received)

    @pl.when(chip < CHIPS // 2)
    def _():
        opposite(orbital(prev2_ref, h), next2_ref)

    @pl.when(chip >= CHIPS // 2)
    def _():
        opposite(orbital(next2_ref, 2 + h), prev2_ref)


def late_send_kernel(prev_ref, next2_ref, prev2_ref, out_ref):
    late_products(True, prev_ref, next2_ref, prev2_ref, 0, out_ref, None)


class Shifted:
    def __init__(self, ref, by):
        self.ref, self.by = ref, by

    def __getitem__(self, key):
        return self.ref[(key[0] - self.by,) + key[1:]]


def late_own_kernel(prev_ref, next2_ref, prev2_ref, early_ref, received, out_ref):
    out_ref[:EARLY] = early_ref[...]
    late_products(
        False, prev_ref, next2_ref, prev2_ref, EARLY, out_ref, Shifted(received, EARLY)
    )


def pair_call(body, operands, slots):
    return pl.pallas_call(
        body,
        out_shape=jax.ShapeDtypeStruct((slots, ROWS, BS), jnp.bfloat16),
        compiler_params=pltpu.CompilerParams(vmem_limit_bytes=PAIR_VMEM),
    )(*operands)


def final_kernel(kinds, domains, eps_occ, mask, both_ref, vir_ref, amp_ref, energy_ref, t_ref):
    first_ref, second_ref = both_ref.at[:ROWS], both_ref.at[ROWS:]
    aux = lax.axis_index("aux")
    orb = lax.axis_index("orb")
    kind = kinds[aux, orb]
    units = [slice(0, BS), slice(BS, 2 * BS)]

    @pl.when(kind == 0)
    def _():
        for j, ref in enumerate((first_ref, second_ref)):
            for i in range(2):
                t_ref[j, i] = ref[units[i]].astype(jnp.float32)

    @pl.when(kind == 1)
    def _():
        for i, ref in enumerate((second_ref, first_ref)):
            for j in range(2):
                t_ref[j, i] = ref[units[j]].astype(jnp.float32).T

    @pl.when(kind == 2)
    def _():
        row = lax.broadcasted_iota(jnp.int32, (BS, BS), 0)
        col = lax.broadcasted_iota(jnp.int32, (BS, BS), 1)
        packed = first_ref[units[0]].astype(jnp.float32)
        flipped = packed.T
        line = first_ref[2 * BS : 2 * BS + EXTRA].astype(jnp.float32)[:1]
        t_ref[0, 0] = jnp.where(row >= col, packed, flipped)
        t_ref[1, 1] = jnp.where(row < col, packed, jnp.where(row > col, flipped, line))
        cross = first_ref[units[1]].astype(jnp.float32)
        t_ref[0, 1] = cross
        t_ref[1, 0] = cross.T

    scale = 1.0 / np.sqrt(np.float32(NAUX))
    for j in range(2):
        jj = 2 * aux + j
        vir_j = vir_ref[pl.ds(domains[jj], 1), :]
        rows = jnp.broadcast_to(vir_j, (BS, BS)).T
        amps = []
        for i in range(2):
            ii = 2 * orb + i
            vir_i = vir_ref[pl.ds(domains[ii], 1), :]
            denominator = rows + vir_i - eps_occ[jj] - eps_occ[ii]
            pair = t_ref[j, i] * scale
            keep = mask[j, i].astype(jnp.float32)
            amp = keep * pair / denominator
            amps.append(amp)
            energy_ref[j, i] = jnp.sum(pair * amp) * (-1.0 / (BS * BS))
        amp_ref[j] = jnp.stack(amps, axis=1).astype(jnp.bfloat16)


def final_call(kinds, domains, eps_occ, mask, both, vir):
    return pl.pallas_call(
        final_kernel,
        grid_spec=pltpu.PrefetchScalarGridSpec(
            num_scalar_prefetch=4,
            grid=(1,),
            in_specs=[
                pl.BlockSpec(both.shape, lambda n, *m: (0, 0)),
                pl.BlockSpec(vir.shape, lambda n, *m: (0, 0)),
            ],
            out_specs=(
                pl.BlockSpec((2, BS, 2, BS), lambda n, *m: (0, 0, 0, 0)),
                pl.BlockSpec(memory_space=pltpu.SMEM),
            ),
            scratch_shapes=[pltpu.VMEM((2, 2, BS, BS), jnp.float32)],
        ),
        out_shape=(
            jax.ShapeDtypeStruct((2, BS, 2, BS), jnp.bfloat16),
            jax.ShapeDtypeStruct((2, 2), jnp.float32),
        ),
        compiler_params=pltpu.CompilerParams(vmem_limit_bytes=PAIR_VMEM),
    )(kinds, domains, eps_occ, mask, both, vir)


def slot_pairs(chip):
    sup = lambda off, l: 2 * ((chip + off) % CHIPS) + l
    pairs = [(sup(0, l), sup(1, m)) for l in range(2) for m in range(2)]
    pairs += [(sup(-1, l), sup(1, m)) for l in range(2) for m in range(2)]
    pairs += [(sup(0, 0), sup(0, 1)), None]
    pairs += [(sup(-1, l), sup(2, m)) for l in range(2) for m in range(2)]
    if chip < CHIPS // 2:
        pairs += [(sup(-2, 0), sup(2, m)) for m in range(2)]
    else:
        pairs += [(sup(2, 1), sup(-2, m)) for m in range(2)]
    return pairs


def delivery():
    pairs = []
    kind = np.full((SLOTS, SLOTS), -1, np.int32)
    for chip in range(CHIPS):
        for slot, pair in enumerate(slot_pairs(chip)):
            for core in range(2):
                u, v = pair or (2 * chip + core,) * 2
                owner = (v, u) if core else (u, v)
                pairs.append((slot * SLOTS + 2 * chip + core, owner[0] * SLOTS + owner[1]))
                kind[owner] = core if pair else 2
    assert (kind >= 0).all()
    return pairs, kind


def shards(integrals, coeffs, domains, eps_occ, eps_vir, pair_mask):
    f32 = jnp.float32
    half = integrals.shape[1] // 2
    integrals = integrals.reshape(-1, 2, half, BS)
    n_orb = 2 * CHIPS
    tie = lax.optimization_barrier
    swap = lambda x: lax.ppermute(x, "orb", [(o, o ^ 1) for o in range(n_orb)])
    up = lambda x: lax.ppermute(x, "orb", [(o, (o + 2) % n_orb) for o in range(n_orb)])
    down = lambda x: lax.ppermute(x, "orb", [(o, (o - 2) % n_orb) for o in range(n_orb)])

    part = half // RINGS
    def add(x, *received):
        return sum((r.astype(f32) for r in received), x).astype(jnp.bfloat16)

    order = (4, 3, 5, 2, 6, 1, 7, 0)
    outs = transform_call(domains, integrals, coeffs, order)
    rows = [slice(first, first + part) for first in range(0, half, part)]
    terms, begin, first_theirs = {}, 0, None
    for group, count in enumerate(GROUPS):
        send, mine = outs[2 * group : 2 * group + 2]
        if first_theirs is None:
            theirs = first_theirs = swap(send)
        else:
            theirs = swap(tie((send, first_theirs))[0])
        values = tie(
            [
                mine[n, r].astype(f32) + theirs[n, r].astype(f32)
                for n in range(count)
                for r in rows
            ]
        )
        for n in range(count):
            terms[order[begin + n]] = values[RINGS * n : RINGS * (n + 1)]
        begin += count

    h = part // 2
    starts = [tie((add(x[:h]), add(x[h:]))) for x in terms[4]]
    sums = [(up(u), down(d)) for u, d in starts]
    for step in (3, 2, 1):
        later = []
        for n, (u, d) in enumerate(sums):
            x, y = terms[step][n], terms[CHIPS - step][n]
            if step == 3:
                u = jnp.concatenate([add(x[:h], u), add(x[h:])], axis=0)
                d = jnp.concatenate([add(y[:h]), add(y[h:], d)], axis=0)
            else:
                u, d = add(x, u), add(y, d)
            u, d = tie((u, d))
            later.append((up(u), down(d)))
        sums = later
    own, prev, next_, prev2, next2 = [], [], [], [], []
    for n, (u, d) in enumerate(sums):
        own.append(tie(add(terms[0][n], u, d)))
        prev.append(up(own[-1]))
        next_.append(down(own[-1]))
    for n in range(RINGS):
        u, d = tie((prev[n], next_[n]))
        prev2.append(up(u))
        next2.append(down(d))
    own, prev, next_, prev2, next2 = (
        jnp.concatenate(x, axis=0) for x in (own, prev, next_, prev2, next2)
    )

    send = pair_call(functools.partial(early_kernel, True), (own, prev, next_), EARLY)
    early = pair_call(
        functools.partial(early_kernel, False), (own, prev, next_, swap(send)), EARLY
    )
    send = pair_call(late_send_kernel, (prev, next2, prev2), SLOTS - EARLY)
    sums = pair_call(late_own_kernel, (prev, next2, prev2, early, swap(send)), SLOTS)
    parts = lax.all_to_all(sums.reshape(SLOTS * ROWS, BS), "aux", 0, 0, tiled=True)
    held = jnp.sum(parts.reshape(SLOTS, ROWS, BS).astype(f32), axis=0).astype(jnp.bfloat16)
    both = jnp.concatenate([held, swap(held)], axis=0)
    pairs, kind = delivery()
    both = lax.ppermute(both, ("aux", "orb"), pairs)
    return final_call(
        jnp.asarray(kind), domains, eps_occ, pair_mask, both, eps_vir.reshape(-1, BS)
    )


def solution(mesh):
    return jax.shard_map(
        shards,
        mesh=mesh,
        in_specs=(P(None, "aux", "orb"), P("orb", None), P(), P(), P(), P("aux", "orb")),
        out_specs=(P("aux", None, "orb", None), P("aux", "orb")),
        check_vma=False,
    )
```
